32 devices in a mesh: row: 4 (over z), col: 8 (over y, x, core).
Axes of the slice: x: 2, y: 2, z: 4, core: 2. Of those that a mesh axis runs over, the one named last changes fastest.
Arguments:
- hidden_in: bfloat16 [1536, 2, 7168], P('row', None, 'col'), may hold values from -16 to 16
- final_gain: float32 [2, 7168], P(None, 'col'), may hold values from 0.25 to 1.75
- unembed: bfloat16 [7168, 32768], P('row', 'col'), may hold values from -2 to 2
- lengths: int32 [8], replicated, may hold values from 1 to 768, 1536 in all
- targets: int32 [1536], P('row'), may hold values from 0 to 32767
- owner: int32 [8], replicated, may hold values from 0 to 7
Outputs:
- owner_table: float32 [8, 3, 8], P('col')
The draws below stay inside these ranges and needn't reach their ends.
Inputs may be any that keep to these rules, and one draw needn't show every extreme that they name: The lengths sum to 1536; the longest is exactly 768.
All inputs are finite; a program needn't handle non-finite values.
Results may differ from the reference program's by a relative error of at most 0.00056.
Values may be sent and summed in bfloat16 or wider, within the bound.
A program may use at most 192 MiB of HBM per device.

```python
import math
import jax
import jax.numpy as jnp
import numpy as np
from jax import lax

D = 7168
VOCAB = 32768
TOK_ROW = 384
TOKENS = 1536
MOST = 768
SEQS = 8
N_COL = 8


def draw_hidden_in(key, part):
    noise_key, row_key, col_key = jax.random.split(key, 3)
    full_shape = (TOKENS, 2, D)
    base_draw = jax.random.normal(noise_key, full_shape, jnp.float32)
    row_scale = jnp.exp(jax.random.uniform(row_key, (TOKENS, 2, 1), jnp.float32, -1.15, 1.15))
    ramp_up = jnp.exp(math.log(3.0) * (jnp.arange(D, dtype=jnp.float32) / D - 0.5))
    col_scale = ramp_up[None, None, :] * jnp.exp(jax.random.uniform(col_key, (1, 2, D), jnp.float32, -0.35, 0.35))
    return jnp.clip(base_draw * row_scale * col_scale, -16.0, 16.0).astype(jnp.bfloat16)


def draw_unembed(key, part):
    base_key = jax.random.fold_in(key, 0)
    ramp_up = jnp.exp(math.log(1.7) * (jnp.arange(VOCAB, dtype=jnp.float32) / VOCAB - 0.5))
    base_draw = jax.random.normal(base_key, (D, VOCAB), jnp.float32) * (3.0 / math.sqrt(D)) * ramp_up[None, :]
    return jnp.clip(base_draw, -2.0, 2.0).astype(jnp.bfloat16)


def plant(result, stream_key, low, top_value):
    spot = [jax.random.randint(jax.random.fold_in(stream_key, axis), (), 0, length) for axis, length in enumerate(result.shape)]
    main_axis = result.shape.index(max(result.shape))
    beside = spot[:main_axis] + [(spot[main_axis] + 1) % result.shape[main_axis]] + spot[main_axis + 1:]
    return result.at[tuple(spot)].set(low).at[tuple(beside)].set(top_value)


def rank_bounds(count, slope):
    weights = [(1 << 20) // math.isqrt(standing ** slope) + 1 for standing in range(1, count + 1)]
    spread = 1 + sum(weights) // (1 << 30)
    return np.cumsum(np.array([max(1, weight // spread) for weight in weights]))


def ranked_ids(stream_key, shape, count, slope):
    listing = rank_bounds(count, slope)
    pick = jax.random.randint(jax.random.fold_in(stream_key, 1), shape, 0, int(listing[count - 1]))
    rank = jnp.searchsorted(jnp.asarray(listing, jnp.int32), pick, side="right")
    return jax.random.permutation(jax.random.fold_in(stream_key, 2), count)[rank].astype(jnp.int32)


def profile(count, total, bound, lean):
    portions = [(1 << 20) // math.isqrt(grade ** lean) + 1 for grade in range(2, count + 1)]
    spare, given = total - bound - (count - 1), [1] * (count - 1)
    while spare > 0:
        candidates = [i for i in range(count - 1) if given[i] < bound]
        pool, remaining = sum([portions[i] for i in candidates]), spare
        for i in candidates:
            more = min(bound - given[i], max(1, remaining * portions[i] // pool), spare)
            given[i] = given[i] + more
            spare = spare - more
    return np.array([bound] + given)


def uneven_parts(stream_key, amount, total, bound, slope):
    if amount == 2:
        one = jax.random.randint(stream_key, (), max(1, total - bound), min(bound, total - 1) + 1)
        return jnp.stack([one, total - one])
    tallies = jnp.asarray(profile(amount, total, bound, slope), jnp.int32)
    twos = (amount - 1) // 2
    donor, receiver = tallies[1:1 + 2 * twos:2], tallies[2:2 + 2 * twos:2]
    margin = jnp.minimum(donor - 1, bound - receiver)
    passed = jax.random.randint(jax.random.fold_in(stream_key, 1), (twos,), 0, 1 << 20) % (margin + 1)
    tallies = tallies.at[1:1 + 2 * twos:2].set(donor - passed).at[2:2 + 2 * twos:2].set(receiver + passed)
    return tallies[jax.random.permutation(jax.random.fold_in(stream_key, 2), amount)]


def setup_inputs(seed: int = 0) -> dict:
    key_of = jax.random.split(jax.random.key(seed), 7)
    return {
        "hidden_in": draw_hidden_in(jax.random.fold_in(key_of[6], 71), 0),
        "final_gain": jnp.clip(1.0 + 0.15 * jax.random.normal(key_of[1], (2, D), jnp.float32), 0.25, 1.75),
        "unembed": draw_unembed(jax.random.fold_in(key_of[6], 71), 0),
        "lengths": uneven_parts(key_of[3], SEQS, TOKENS, MOST, 1).astype(jnp.int32),
        "targets": plant(ranked_ids(key_of[4], (TOKENS,), VOCAB, 2), jax.random.fold_in(key_of[4], 3), 0, VOCAB - 1).astype(jnp.int32),
        "owner": plant(jax.random.randint(key_of[5], (SEQS,), 0, N_COL), jax.random.fold_in(key_of[5], 1), 0, N_COL - 1).astype(jnp.int32),
    }


EPS = 1e-05

def reference(hidden_in, final_gain, unembed, lengths, targets, owner):
    stream = hidden_in.astype(jnp.float32)
    normed = (stream * lax.rsqrt(lax.optimization_barrier(jnp.mean(stream * stream, axis=2, keepdims=True)) + EPS) * final_gain[None, :, :]).astype(jnp.bfloat16)
    block_count = TOKENS // TOK_ROW
    vocab_ids = jnp.arange(VOCAB, dtype=jnp.int32)

    def score(inputs):
        block_rows, block_targets = inputs
        results = []
        for model_index in range(2):
            logits = jnp.dot(block_rows[:, model_index], unembed, preferred_element_type=jnp.float32)
            row_max = lax.optimization_barrier(jnp.max(logits, axis=1))
            exp_total = lax.optimization_barrier(jnp.sum(jnp.exp(logits - row_max[:, None]), axis=1))
            picked = lax.optimization_barrier(jnp.sum(jnp.where(block_targets[:, None] == vocab_ids[None, :], logits, 0.0), axis=1))
            results.append(picked - (row_max + jnp.log(exp_total)))
        return results[0] - results[1]
    log_ratio = lax.map(score, (normed.reshape(block_count, TOK_ROW, 2, D), targets.reshape(block_count, TOK_ROW))).reshape(TOKENS)
    token_index = jnp.arange(TOKENS, dtype=jnp.int32)
    seq_ends = jnp.cumsum(lengths).astype(jnp.int32)
    segment = lax.optimization_barrier(jnp.sum((seq_ends[None, :] <= token_index[:, None]).astype(jnp.int32), axis=1))
    member = segment[:, None] == jnp.arange(SEQS, dtype=jnp.int32)[None, :]
    ratio_sums = lax.optimization_barrier(jnp.sum(jnp.where(member, log_ratio[:, None], 0.0), axis=0))
    squares = lax.optimization_barrier(jnp.sum(jnp.where(member, (log_ratio * log_ratio)[:, None], 0.0), axis=0))
    ratio_max = lax.optimization_barrier(jnp.max(jnp.where(member, log_ratio[:, None], -1e+30), axis=0))
    seq_stats = jnp.stack([ratio_sums, squares, ratio_max])
    owned = owner[None, :] == jnp.arange(N_COL, dtype=jnp.int32)[:, None]
    return jnp.where(owned[:, None, :], seq_stats[None], 0.0)
```

```python
import jax
import jax.numpy as jnp
from jax import lax
from jax.sharding import PartitionSpec as P

EPS = 1e-05


def per_device(n_row, n_col, hidden_in, final_gain, unembed, lengths, targets, owner):
    tok_rows = hidden_in.shape[0]
    width = hidden_in.shape[2] * n_col
    vocab_cols = unembed.shape[1] // n_row
    tokens = tok_rows * n_row
    row_index = lax.axis_index("row")
    col_index = lax.axis_index("col")
    stream = hidden_in.astype(jnp.float32)
    square_sum = lax.psum(jnp.sum(stream * stream, axis=2), "col")
    normed = (
        stream * lax.rsqrt(square_sum[:, :, None] / width + EPS) * final_gain[None, :, :]
    ).astype(jnp.bfloat16)
    normed = normed.reshape(tok_rows * 2, hidden_in.shape[2])
    columns = lax.all_to_all(unembed, "row", split_axis=1, concat_axis=0, tiled=True)
    features = lax.all_gather(normed, "row", axis=0, tiled=True)
    features = lax.all_gather(features, "col", axis=0, tiled=False)
    features = features.transpose(1, 0, 2).reshape(tokens * 2, width)
    logits = jnp.dot(features, columns, preferred_element_type=jnp.float32)
    row_max = jnp.max(logits, axis=1)
    exp_total = jnp.sum(jnp.exp(logits - row_max[:, None]), axis=1)
    all_targets = lax.all_gather(targets, "row", axis=0, tiled=True)
    first = (col_index * n_row + row_index) * vocab_cols
    vocab_ids = first + jnp.arange(vocab_cols, dtype=jnp.int32)
    wanted = jnp.repeat(all_targets, 2)
    picked = jnp.sum(jnp.where(wanted[:, None] == vocab_ids[None, :], logits, 0.0), axis=1)
    max_logit = lax.pmax(row_max, ("row", "col"))
    exp_total, picked = lax.psum(
        (exp_total * jnp.exp(row_max - max_logit), picked), ("row", "col")
    )
    logp = (picked - (max_logit + jnp.log(exp_total))).reshape(tokens, 2)
    log_ratio = logp[:, 0] - logp[:, 1]
    token_index = jnp.arange(tokens, dtype=jnp.int32)
    seq_ends = jnp.cumsum(lengths)
    segment = jnp.sum((seq_ends[None, :] <= token_index[:, None]).astype(jnp.int32), axis=1)
    member = segment[:, None] == jnp.arange(lengths.shape[0], dtype=jnp.int32)[None, :]
    ratio_sums = jnp.sum(jnp.where(member, log_ratio[:, None], 0.0), axis=0)
    squares = jnp.sum(jnp.where(member, (log_ratio * log_ratio)[:, None], 0.0), axis=0)
    ratio_max = jnp.max(jnp.where(member, log_ratio[:, None], -1e30), axis=0)
    seq_stats = jnp.stack([ratio_sums, squares, ratio_max])
    owned = owner == col_index
    return jnp.where(owned[None, :], seq_stats, 0.0)[None]


def solution(mesh):
    import functools
    in_specs = (P("row", None, "col"), P(None, "col"), P("row", "col"), P(), P("row"), P())
    return jax.shard_map(
        functools.partial(per_device, mesh.shape["row"], mesh.shape["col"]),
        mesh=mesh,
        in_specs=in_specs,
        out_specs=P("col", None, None),
        check_vma=False,
    )
```

```python
import functools

import jax
import jax.numpy as jnp
from jax import lax
from jax.experimental import pallas as pl
from jax.experimental.pallas import tpu as pltpu
from jax.sharding import PartitionSpec as P

EPS = 1e-05
LANES = 128


def score_kernel(n_row, row_ref, features_ref, wanted_ref, *refs):
    pieces, stats_ref = refs[:-1], refs[-1]
    blocks, rows, depth = features_ref.shape
    vocab_cols = pieces[0].shape[1]
    share = blocks // n_row
    logits = jnp.zeros((rows, vocab_cols), jnp.float32)
    for shift in range(n_row):
        source = lax.rem(row_ref[0] + n_row - shift, n_row)
        for part in range(share):
            logits += jnp.dot(
                features_ref[source * share + part],
                pieces[shift][pl.ds(part * depth, depth), :],
                preferred_element_type=jnp.float32,
            )
    row_max = jnp.max(logits, axis=1, keepdims=True)
    exp_total = jnp.sum(jnp.exp(logits - row_max), axis=1, keepdims=True)
    vocab_ids = lax.broadcasted_iota(jnp.int32, (rows, vocab_cols), 1)
    picked = jnp.sum(
        jnp.where(wanted_ref[...] == vocab_ids, logits, 0.0), axis=1, keepdims=True
    )
    lane = lax.broadcasted_iota(jnp.int32, (rows, LANES), 1)
    stats_ref[...] = jnp.where(lane == 0, row_max, jnp.where(lane == 1, exp_total, picked))


def score(n_row, row_index, features, pieces, wanted):
    blocks, tokens, depth = features.shape
    vocab_cols = pieces[0].shape[1]
    rows = 256
    return pl.pallas_call(
        functools.partial(score_kernel, n_row),
        grid=(tokens // rows,),
        out_shape=jax.ShapeDtypeStruct((tokens, LANES), jnp.float32),
        in_specs=[
            pl.BlockSpec(memory_space=pltpu.SMEM),
            pl.BlockSpec((blocks, rows, depth), lambda i: (0, i, 0)),
            pl.BlockSpec((rows, 1), lambda i: (i, 0)),
            *(pl.BlockSpec(piece.shape, lambda i: (0, 0)) for piece in pieces),
        ],
        out_specs=pl.BlockSpec((rows, LANES), lambda i: (i, 0)),
        compiler_params=pltpu.CompilerParams(vmem_limit_bytes=56 << 20),
        cost_estimate=pl.CostEstimate(
            flops=2 * tokens * blocks * depth * vocab_cols,
            bytes_accessed=2 * (features.size + n_row * pieces[0].size),
            transcendentals=tokens * vocab_cols,
        ),
    )(row_index[None], features, wanted, *pieces)


def cut_columns(n_row, row_index, unembed, vocab_cols):
    return [
        lax.dynamic_slice_in_dim(
            unembed, lax.rem(row_index + k, n_row) * vocab_cols, vocab_cols, axis=1
        )
        for k in range(n_row)
    ]


def send_on(n_row, shift, piece):
    return lax.ppermute(piece, "row", [(r, (r + shift) % n_row) for r in range(n_row)])


def per_device(n_row, n_col, hidden_in, final_gain, unembed, lengths, targets, owner):
    tok_rows = hidden_in.shape[0]
    width = hidden_in.shape[2] * n_col
    vocab_cols = unembed.shape[1] // n_row
    tokens = tok_rows * n_row
    row_index = lax.axis_index("row")
    col_index = lax.axis_index("col")
    stream = hidden_in.astype(jnp.float32)
    square_sum = lax.psum(jnp.sum(stream * stream, axis=2), "col")
    normed = (
        stream * lax.rsqrt(square_sum[:, :, None] / width + EPS) * final_gain[None, :, :]
    ).astype(jnp.bfloat16)
    normed = normed.reshape(tok_rows * 2, hidden_in.shape[2])
    cuts = cut_columns(n_row, row_index, unembed, vocab_cols)
    normed, *cuts = lax.optimization_barrier((normed, *cuts))
    nearest = send_on(n_row, 1, cuts[1])
    features = lax.all_gather(normed, "row", axis=0, tiled=True)
    features, nearest = lax.optimization_barrier((features, nearest))
    pieces = [cuts[0], nearest, *(send_on(n_row, k, cuts[k]) for k in range(2, n_row))]
    features = lax.all_gather(features, "col", axis=0, tiled=False)
    wanted = jnp.repeat(lax.all_gather(targets, "row", axis=0, tiled=True), 2)
    first = (col_index * n_row + row_index) * vocab_cols
    stats = score(n_row, row_index, features, pieces, (wanted - first)[:, None])
    stats = lax.all_gather(stats[:, :3].T, ("row", "col"), axis=0, tiled=False)
    max_logit = jnp.max(stats[:, 0], axis=0)
    exp_total = jnp.sum(stats[:, 1] * jnp.exp(stats[:, 0] - max_logit[None]), axis=0)
    picked = jnp.sum(stats[:, 2], axis=0)
    logp = (picked - (max_logit + jnp.log(exp_total))).reshape(tokens, 2)
    log_ratio = logp[:, 0] - logp[:, 1]
    token_index = jnp.arange(tokens, dtype=jnp.int32)
    seq_ends = jnp.cumsum(lengths)
    segment = jnp.sum((seq_ends[None, :] <= token_index[:, None]).astype(jnp.int32), axis=1)
    member = segment[:, None] == jnp.arange(lengths.shape[0], dtype=jnp.int32)[None, :]
    ratio_sums = jnp.sum(jnp.where(member, log_ratio[:, None], 0.0), axis=0)
    squares = jnp.sum(jnp.where(member, (log_ratio * log_ratio)[:, None], 0.0), axis=0)
    ratio_max = jnp.max(jnp.where(member, log_ratio[:, None], -1e30), axis=0)
    seq_stats = jnp.stack([ratio_sums, squares, ratio_max])
    owned = owner == col_index
    return jnp.where(owned[None, :], seq_stats, 0.0)[None]


def solution(mesh):
    in_specs = (P("row", None, "col"), P(None, "col"), P("row", "col"), P(), P("row"), P())
    return jax.shard_map(
        functools.partial(per_device, mesh.shape["row"], mesh.shape["col"]),
        mesh=mesh,
        in_specs=in_specs,
        out_specs=P("col", None, None),
        check_vma=False,
    )
```

```python
import functools

import jax
import jax.numpy as jnp
from jax import lax
from jax.experimental import pallas as pl
from jax.experimental.pallas import tpu as pltpu
from jax.sharding import PartitionSpec as P

EPS = 1e-05
LANES = 128


def score_kernel(n_row, spans, row_ref, features_ref, wanted_ref, *refs):
    pieces, stats_ref = refs[:-1], refs[-1]
    blocks, rows, depth = features_ref.shape
    vocab_cols = pieces[0].shape[1]
    share = blocks // n_row
    logits = jnp.zeros((rows, vocab_cols), jnp.float32)
    for (shift, first), piece in zip(spans, pieces):
        source = lax.rem(row_ref[0] + n_row - shift, n_row)
        for part in range(piece.shape[0] // depth):
            logits += jnp.dot(
                features_ref[source * share + first + part],
                piece[pl.ds(part * depth, depth), :],
                preferred_element_type=jnp.float32,
            )
    row_max = jnp.max(logits, axis=1, keepdims=True)
    exp_total = jnp.sum(jnp.exp(logits - row_max), axis=1, keepdims=True)
    vocab_ids = lax.broadcasted_iota(jnp.int32, (rows, vocab_cols), 1)
    picked = jnp.sum(
        jnp.where(wanted_ref[...] == vocab_ids, logits, 0.0), axis=1, keepdims=True
    )
    lane = lax.broadcasted_iota(jnp.int32, (rows, LANES), 1)
    stats_ref[...] = jnp.where(lane == 0, row_max, jnp.where(lane == 1, exp_total, picked))


def score(n_row, row_index, features, spans, pieces, wanted):
    blocks, tokens, depth = features.shape
    vocab_cols = pieces[0].shape[1]
    rows = 256
    return pl.pallas_call(
        functools.partial(score_kernel, n_row, spans),
        grid=(tokens // rows,),
        out_shape=jax.ShapeDtypeStruct((tokens, LANES), jnp.float32),
        in_specs=[
            pl.BlockSpec(memory_space=pltpu.SMEM),
            pl.BlockSpec((blocks, rows, depth), lambda i: (0, i, 0)),
            pl.BlockSpec((rows, 1), lambda i: (i, 0)),
            *(pl.BlockSpec(piece.shape, lambda i: (0, 0)) for piece in pieces),
        ],
        out_specs=pl.BlockSpec((rows, LANES), lambda i: (i, 0)),
        compiler_params=pltpu.CompilerParams(vmem_limit_bytes=56 << 20),
        cost_estimate=pl.CostEstimate(
            flops=2 * tokens * blocks * depth * vocab_cols,
            bytes_accessed=2 * (features.size + sum(piece.size for piece in pieces)),
            transcendentals=tokens * vocab_cols,
        ),
    )(row_index[None], features, wanted, *pieces)


def cut_columns(n_row, row_index, unembed, vocab_cols):
    return [
        lax.dynamic_slice_in_dim(
            unembed, lax.rem(row_index + k, n_row) * vocab_cols, vocab_cols, axis=1
        )
        for k in range(n_row)
    ]


def send_on(n_row, shift, piece):
    return lax.ppermute(piece, "row", [(r, (r + shift) % n_row) for r in range(n_row)])


def per_device(n_row, n_col, hidden_in, final_gain, unembed, lengths, targets, owner):
    tok_rows = hidden_in.shape[0]
    width = hidden_in.shape[2] * n_col
    vocab_cols = unembed.shape[1] // n_row
    tokens = tok_rows * n_row
    row_index = lax.axis_index("row")
    col_index = lax.axis_index("col")
    stream = hidden_in.astype(jnp.float32)
    cuts = cut_columns(n_row, row_index, unembed, vocab_cols)
    split = max(1, n_col // n_row // 2) * hidden_in.shape[2]
    cuts = [cuts[0], cuts[1][:split], cuts[1][split:], *cuts[2:]]
    square_sum, *cuts = lax.optimization_barrier((jnp.sum(stream * stream, axis=2), *cuts))
    square_sum = lax.psum(square_sum, "col")
    normed = (
        stream * lax.rsqrt(square_sum[:, :, None] / width + EPS) * final_gain[None, :, :]
    ).astype(jnp.bfloat16)
    normed = normed.reshape(tok_rows * 2, hidden_in.shape[2])
    normed, early = lax.optimization_barrier((normed, send_on(n_row, 1, cuts[1])))
    late = send_on(n_row, 1, cuts[2])
    features = lax.all_gather(normed, "row", axis=0, tiled=True)
    features, late = lax.optimization_barrier((features, late))
    others = [send_on(n_row, k, cuts[k + 1]) for k in range(2, n_row)]
    pieces = [cuts[0], early, late, *others]
    spans = [(0, 0), (1, 0), (1, split // hidden_in.shape[2])]
    spans += [(k, 0) for k in range(2, n_row)]
    features = lax.all_gather(features, "col", axis=0, tiled=False)
    wanted = jnp.repeat(lax.all_gather(targets, "row", axis=0, tiled=True), 2)
    first = (col_index * n_row + row_index) * vocab_cols
    stats = score(n_row, row_index, features, spans, pieces, (wanted - first)[:, None])
    stats = lax.all_gather(stats[:, :3].T, ("row", "col"), axis=0, tiled=False)
    max_logit = jnp.max(stats[:, 0], axis=0)
    exp_total = jnp.sum(stats[:, 1] * jnp.exp(stats[:, 0] - max_logit[None]), axis=0)
    picked = jnp.sum(stats[:, 2], axis=0)
    logp = (picked - (max_logit + jnp.log(exp_total))).reshape(tokens, 2)
    log_ratio = logp[:, 0] - logp[:, 1]
    token_index = jnp.arange(tokens, dtype=jnp.int32)
    seq_ends = jnp.cumsum(lengths)
    segment = jnp.sum((seq_ends[None, :] <= token_index[:, None]).astype(jnp.int32), axis=1)
    member = segment[:, None] == jnp.arange(lengths.shape[0], dtype=jnp.int32)[None, :]
    ratio_sums = jnp.sum(jnp.where(member, log_ratio[:, None], 0.0), axis=0)
    squares = jnp.sum(jnp.where(member, (log_ratio * log_ratio)[:, None], 0.0), axis=0)
    ratio_max = jnp.max(jnp.where(member, log_ratio[:, None], -1e30), axis=0)
    seq_stats = jnp.stack([ratio_sums, squares, ratio_max])
    owned = owner == col_index
    return jnp.where(owned[None, :], seq_stats, 0.0)[None]


def solution(mesh):
    in_specs = (P("row", None, "col"), P(None, "col"), P("row", "col"), P(), P("row"), P())
    return jax.shard_map(
        functools.partial(per_device, mesh.shape["row"], mesh.shape["col"]),
        mesh=mesh,
        in_specs=in_specs,
        out_specs=P("col", None, None),
        check_vma=False,
    )
```
